768 devices in a mesh: img: 192 (over y, z, x_hi), txt: 4 (over x_lo, core).
Axes of the slice: x: 4 (x_hi: 2, x_lo: 2; x = x_hi * 2 + x_lo), y: 8, z: 12, core: 2. Of those that a mesh axis runs over, the one named last changes fastest.
Arguments:
- images: bfloat16 [147456, 1152], P(('img', 'txt')), may hold values from -0.1875 to 0.1875
- texts: bfloat16 [147456, 1152], P(('img', 'txt')), may hold values from -0.1875 to 0.1875
- log_temp: float32 [], replicated, may hold values from 1.8 to 2.6
- bias: float32 [], replicated, may hold values from -4 to -2
Outputs:
- text_loss: float32 [147456], P(('img', 'txt'))
- image_grad: float32 [147456, 1152], P(('img', 'txt'))
- text_grad: float32 [147456, 1152], P(('img', 'txt'))
The draws below stay inside these ranges and needn't reach their ends.
All inputs are finite; a program needn't handle non-finite values.
Results may differ from the reference program's by a relative error of at most 0.0043.
Values may be sent and summed in bfloat16 or wider, within the bound.
No kernel may reach another device: no remote copies, remote signals or barrier semaphores. Data moves between devices by JAX's collectives and lax.ppermute only.
A program may use at most 32 MiB of HBM per device.

```python
import jax
import jax.numpy as jnp
from jax import lax

D = 1152
ROWS = 192
VISITS = 4
BATCH = 147456
N_IMG = 192
N_TXT = 4


def levels(stream_key, dims, pieces, least, high):
    def one(position, parts):
        draws = jax.random.uniform(jax.random.fold_in(jax.random.fold_in(stream_key, 6), position), (parts,), jnp.float32, least / len(pieces), high / len(pieces))
        return jnp.repeat(jnp.exp(draws), dims[position] // parts).reshape((-1,) + (1,) * (len(dims) - position - 1))

    gain = one(*pieces[0])
    for cut in pieces[1:]:
        gain = gain * one(*cut)
    return gain


def noise(key, dims, scale, reach, shards=(), kind=jnp.bfloat16):
    result = jax.random.normal(key, dims, jnp.float32) * scale
    if len(shards) > 0:
        result = levels(key, dims, shards, -0.22, 0.18) * result
    return jnp.clip(result, min=-reach, max=reach).astype(kind)


def setup_inputs(seed: int = 0) -> dict:
    splits = jax.random.split(jax.random.key(seed), 5)
    return {
        "images": noise(splits[0], (BATCH, D), 0.03, 0.1875, ((0, 768),)),
        "texts": noise(splits[1], (BATCH, D), 0.03, 0.1875, ((0, 768),)),
        "log_temp": jnp.clip(jax.random.uniform(splits[2], (), jnp.float32, 1.8, 2.6), 1.8, 2.6),
        "bias": jnp.clip(jax.random.uniform(splits[3], (), jnp.float32, -4.0, -2.0), -4.0, -2.0),
    }


EPSILON = 1e-06

def unit_rows(values):
    wide = values.astype(jnp.float32)
    length = jnp.sqrt(lax.optimization_barrier(jnp.sum(wide * wide, axis=-1, keepdims=True)) + EPSILON)
    return (wide / length, length)

def reference(images, texts, log_temp, bias):
    temper = jnp.exp(log_temp)
    image_unit, image_length = unit_rows(images)
    text_unit, text_length = unit_rows(texts)
    image_half = image_unit.astype(jnp.bfloat16)
    text_half = text_unit.astype(jnp.bfloat16)
    batch = images.shape[0]
    group = ROWS * N_TXT
    image_blocks = image_half.astype(jnp.float32).reshape(N_IMG, group, D)
    text_blocks = text_half.astype(jnp.float32).reshape(N_IMG, group, D)
    diagonal = jnp.eye(group, dtype=jnp.float32)
    image_dir = jnp.zeros((N_IMG, group, D), jnp.float32)
    text_dir = jnp.zeros((N_IMG, group, D), jnp.float32)
    loss_sum = jnp.zeros((N_IMG, group), jnp.float32)
    for step in range(VISITS):
        seen = jnp.roll(text_blocks, step, axis=0)
        logits = temper * jnp.einsum('ngd,nrd->ngr', image_blocks, seen) + bias
        if step == 0:
            labels = (2.0 * diagonal - 1.0)[None, :, :]
        else:
            labels = -jnp.ones((1, group, group), jnp.float32)
        margin = -labels * logits
        losses = lax.optimization_barrier(jnp.sum(jax.nn.softplus(margin), axis=1))
        slopes = (-labels * jax.nn.sigmoid(margin)).astype(jnp.bfloat16).astype(jnp.float32)
        image_dir = image_dir + temper * jnp.einsum('ngr,nrd->ngd', slopes, seen)
        text_part = temper * jnp.einsum('ngr,ngd->nrd', slopes, image_blocks)
        text_dir = text_dir + jnp.roll(text_part, -step, axis=0)
        loss_sum = loss_sum + jnp.roll(losses, -step, axis=0)
    image_dir = image_dir.reshape(batch, D)
    text_dir = text_dir.reshape(batch, D)
    text_loss = loss_sum.reshape(batch) / (VISITS * group)
    image_grad = (image_dir - image_unit * lax.optimization_barrier(jnp.sum(image_unit * image_dir, axis=-1, keepdims=True))) / image_length
    text_grad = (text_dir - text_unit * lax.optimization_barrier(jnp.sum(text_unit * text_dir, axis=-1, keepdims=True))) / text_length
    return (text_loss, image_grad, text_grad)
```

```python
import functools

import jax
import jax.numpy as jnp
from jax import lax
from jax.experimental import pallas as pl
from jax.experimental.pallas import tpu as pltpu

EPSILON = 1e-06
VISITS = 4
TAIL = 16
AXES = ("img", "txt")
F32, BF16 = jnp.float32, jnp.bfloat16
VMEM = pl.BlockSpec(memory_space=pltpu.VMEM)
SMEM = pl.BlockSpec(memory_space=pltpu.SMEM)
PARAMS = pltpu.CompilerParams(vmem_limit_bytes=48 * 1024 * 1024)


def moved(value, lines, up=0, flip=0, other=0, odd_only=False):
    route = []
    for line in range(lines):
        for x in range(4):
            if odd_only and x < 2:
                continue
            for c in range(2):
                here = line * 8 + x * 2 + c
                there = (line + up) % lines * 8 + (x ^ flip) * 2 + (c ^ other)
                route.append((here, there))
    return lax.ppermute(value, AXES, route)


def unit_of(ref):
    wide = ref[...].astype(F32)
    length = jnp.sqrt(jnp.sum(wide * wide, axis=-1, keepdims=True) + EPSILON)
    return wide / length, length


def norm_kernel(images, texts, image_half, text_half):
    image_half[...] = unit_of(images)[0].astype(BF16)
    text_half[...] = unit_of(texts)[0].astype(BF16)


def tail_of(loss):
    rows = lax.broadcasted_iota(jnp.int32, (TAIL, loss.shape[1]), 0)
    wide = jnp.broadcast_to(loss, rows.shape)
    high = wide.astype(BF16).astype(F32)
    return jnp.where(rows == 0, high, jnp.where(rows == 1, wide - high, 0.0)).astype(BF16)


def pairs_kernel(
    scalars, odd, i0, i1, i2, i3, ao, as_, bo, bs, co, cs,
    image_own, image_1, image_2, image_3, text_own, text_send, loss_own,
    ih, tt, p, sums,
):
    r, width = i0.shape
    n = 2 * r
    temper, bias = scalars[0], scalars[1]
    for k, ref in enumerate((i0, i1, i2, i3, )):
        ih[pl.ds(k * r, r), :] = ref[...]
    for k, ref in enumerate((ao, as_, bo, bs)):
        tt[pl.ds(k * r, r), :] = ref[...]

    @pl.when(odd[0] == 0)
    def _():
        tt[pl.ds(2 * n, r), :] = ao[...]
        tt[pl.ds(2 * n + r, r), :] = as_[...]

    @pl.when(odd[0] != 0)
    def _():
        tt[pl.ds(2 * n, r), :] = co[...]
        tt[pl.ds(2 * n + r, r), :] = cs[...]

    sums[...] = jnp.zeros_like(sums)
    step = 2 * n // 3
    for half in range(2):
        for piece in range(3):
            at = half * n + piece * step
            logits = bias + temper * lax.dot_general(
                ih[pl.ds(half * n, n), :],
                tt[pl.ds(at, step), :],
                (((1,), (1,)), ((), ())),
                preferred_element_type=F32,
            )
            if at < r:
                rows = lax.broadcasted_iota(jnp.int32, logits.shape, 0)
                cols = lax.broadcasted_iota(jnp.int32, logits.shape, 1) + at
                positive = (rows == cols) & (cols < r)
                margin = jnp.where(positive, -logits, logits)
            else:
                margin = logits
            grown = jnp.exp(margin)
            whole = 1.0 + grown
            slope = grown / whole
            losses = jnp.where(
                grown < 0.00390625,
                grown * (1.0 - grown * (0.5 - grown * (1.0 / 3.0))),
                jnp.log(whole),
            )
            if at < r:
                slope = jnp.where(positive, -slope, slope)
            p[pl.ds(half * n, n), pl.ds(at, step)] = slope.astype(BF16)
            sums[:, pl.ds(at, step)] += jnp.sum(losses.reshape(n // 8, 8, step), axis=0)

    nn = (((1,), (0,)), ((), ()))
    tn = (((0,), (0,)), ((), ()))

    def text_part(place, first, rows, at):
        part = lax.dot_general(
            p[pl.ds(first, rows), pl.ds(at, n)],
            ih[pl.ds(first, rows), :],
            tn,
            preferred_element_type=F32,
        )
        text_own[place] = part[:r]
        text_send[place, pl.ds(0, r), :] = part[r:].astype(BF16)
        loss = jnp.sum(sums[:, pl.ds(at, n)], axis=0, keepdims=True)
        loss = jnp.broadcast_to(loss, (8, n))
        loss_own[place] = loss
        text_send[place, pl.ds(r, TAIL), :] = jnp.zeros((TAIL, width), BF16)
        text_send[place, pl.ds(r, TAIL), pl.ds(0, n)] = tail_of(pltpu.roll(loss, r, 1)[:1])

    text_part(0, 0, 2 * n, n)
    text_part(1, n, n, 2 * n)
    text_part(2, 0, n, 0)
    other = lax.dot_general(
        p[pl.ds(n, n), pl.ds(n, 2 * n)], tt[pl.ds(n, 2 * n), :], nn, preferred_element_type=F32
    )
    image_2[...] = other[:r].astype(BF16)
    image_3[...] = other[r:].astype(BF16)
    own = lax.dot_general(
        p[pl.ds(0, n), pl.ds(0, 2 * n)], tt[pl.ds(0, 2 * n), :], nn, preferred_element_type=F32
    )
    image_own[...] = own[:r]
    image_1[...] = own[r:].astype(BF16)


def join_kernel(text_own, got, loss_own, b_back, c_back):
    r = text_own.shape[1]
    for place, out in ((0, b_back), (1, c_back)):
        out[pl.ds(0, r), :] = (text_own[place] + got[place, pl.ds(0, r), :].astype(F32)).astype(BF16)
        tail = got[place, pl.ds(r, TAIL), :].astype(F32)
        n = loss_own.shape[2]
        loss = loss_own[place][:1] + tail[0:1, :n] + tail[1:2, :n]
        out[pl.ds(r, TAIL), :] = jnp.zeros((TAIL, out.shape[1]), BF16)
        out[pl.ds(r, TAIL), pl.ds(0, n)] = tail_of(loss)


def tangent(total, ref, temper):
    unit, length = unit_of(ref)
    total = temper * total
    return (total - unit * jnp.sum(unit * total, axis=-1, keepdims=True)) / length


def image_end_kernel(scalars, images, own, a, b, c, grad):
    total = own[...] + a[...].astype(F32) + b[...].astype(F32) + c[...].astype(F32)
    grad[...] = tangent(total, images, scalars[0])


def text_end_kernel(scalars, odd, texts, own, got, loss_own, b_got, c_got, grad, loss):
    r = texts.shape[0]
    n = loss_own.shape[2]
    even = odd[0] == 0

    def here(place):
        rows = own[place] + got[place, pl.ds(0, r), :].astype(F32)
        tail = got[place, pl.ds(r, TAIL), :].astype(F32)
        return rows, loss_own[place][:1] + tail[0:1, :n] + tail[1:2, :n]

    total, sums = here(2)
    more, more_sums = here(1)
    total = total + jnp.where(even, more, 0.0)
    sums = sums + jnp.where(even, more_sums, 0.0)
    for ref in (b_got, c_got):
        total = total + ref[pl.ds(0, r), :].astype(F32)
        tail = ref[pl.ds(r, TAIL), :].astype(F32)
        sums = sums + tail[0:1, :n] + tail[1:2, :n]
    grad[...] = tangent(total, texts, scalars[0])
    loss[...] = jnp.broadcast_to(sums / (VISITS * 4 * r), loss.shape)


def on_device(lines, images, texts, log_temp, bias):
    r, width = images.shape
    n = 2 * r
    shape = jax.ShapeDtypeStruct
    send = functools.partial(moved, lines=lines)
    scalars = jnp.stack([jnp.exp(log_temp), bias])
    odd = jnp.reshape(lax.axis_index("img") % 2, (1,)).astype(jnp.int32)
    half = shape((r, width), BF16)
    image_half, text_half = pl.pallas_call(
        norm_kernel, out_shape=(half, half), in_specs=[VMEM] * 2, out_specs=(VMEM,) * 2, compiler_params=PARAMS
    )(images, texts)

    text_sib = send(text_half, other=1)
    image_1 = send(image_half, flip=1)
    image_3 = send(image_half, flip=3)
    b_own = send(text_half, up=1)
    image_2 = send(image_half, flip=2)
    c_own = send(text_half, up=2, odd_only=True)
    b_sib = send(b_own, other=1)
    c_sib = send(c_own, other=1)

    long = shape((r, width), F32)
    sent = shape((3, r + TAIL, width), BF16)
    own, out_1, out_2, out_3, text_own, text_send, loss_own = pl.pallas_call(
        pairs_kernel,
        out_shape=(long, half, half, half, shape((3, r, width), F32), sent, shape((3, 8, n), F32)),
        in_specs=[SMEM] * 2 + [VMEM] * 10,
        out_specs=(VMEM,) * 7,
        scratch_shapes=[
            pltpu.VMEM((2 * n, width), BF16),
            pltpu.VMEM((3 * n, width), BF16),
            pltpu.VMEM((2 * n, 3 * n), BF16),
            pltpu.VMEM((8, 3 * n), F32),
        ],
        compiler_params=PARAMS,
    )(scalars, odd, image_half, image_1, image_2, image_3, text_half, text_sib, b_own, b_sib, c_own, c_sib)

    got = send(text_send, other=1)
    back_2 = send(out_2, flip=2)
    back_3 = send(out_3, flip=3)
    back_1 = send(out_1, flip=1)
    back = shape((r + TAIL, width), BF16)
    b_back, c_back = pl.pallas_call(
        join_kernel, out_shape=(back, back), in_specs=[VMEM] * 3, out_specs=(VMEM,) * 2, compiler_params=PARAMS
    )(text_own, got, loss_own)
    c_got = send(c_back, up=-2, odd_only=True)
    b_got = send(b_back, up=-1)
    image_grad = pl.pallas_call(
        image_end_kernel, out_shape=long, in_specs=[SMEM] + [VMEM] * 5, out_specs=VMEM, compiler_params=PARAMS
    )(scalars, images, own, back_1, back_2, back_3)
    text_grad, loss = pl.pallas_call(
        text_end_kernel,
        out_shape=(long, shape((8, n), F32)),
        in_specs=[SMEM] * 2 + [VMEM] * 6,
        out_specs=(VMEM,) * 2,
        compiler_params=PARAMS,
    )(scalars, odd, texts, text_own, got, loss_own, b_got, c_got)
    return loss[0, :r], image_grad, text_grad


def solution(mesh):
    from jax.sharding import PartitionSpec as P

    lines = mesh.shape["img"] // 2
    rows = P(AXES, None)
    return jax.shard_map(
        functools.partial(on_device, lines),
        mesh=mesh,
        in_specs=(rows, rows, P(), P()),
        out_specs=(P(AXES), rows, rows),
        check_vma=False,
    )
```

```python
import functools

import jax
import jax.numpy as jnp
from jax import lax
from jax.experimental import pallas as pl
from jax.experimental.pallas import tpu as pltpu

EPSILON = 1e-06
VISITS = 4
TAIL = 16
AXES = ("img", "txt")
F32, BF16 = jnp.float32, jnp.bfloat16
NT = (((1,), (1,)), ((), ()))
NN = (((1,), (0,)), ((), ()))
TN = (((0,), (0,)), ((), ()))
HBM = pl.BlockSpec(memory_space=pltpu.HBM)
VMEM = pl.BlockSpec(memory_space=pltpu.VMEM)
SMEM = pl.BlockSpec(memory_space=pltpu.SMEM)
PARAMS = pltpu.CompilerParams(vmem_limit_bytes=48 * 1024 * 1024)


def moved(value, lines, up=0, flip=0, other=0, odd_only=False):
    route = []
    for line in range(lines):
        for x in range(4):
            if odd_only and x < 2:
                continue
            for c in range(2):
                here = line * 8 + x * 2 + c
                there = (line + up) % lines * 8 + (x ^ flip) * 2 + (c ^ other)
                route.append((here, there))
    return lax.ppermute(value, AXES, route)


def unit_of(ref):
    wide = ref[...].astype(F32)
    square = jnp.sum(wide * wide, axis=-1, keepdims=True) + EPSILON
    scale = 1.0 / jnp.sqrt(square)
    return wide * scale, scale


def half_of(ref):
    return unit_of(ref)[0].astype(BF16)


def tail_of(loss):
    rows = lax.broadcasted_iota(jnp.int32, (TAIL, loss.shape[1]), 0)
    wide = jnp.broadcast_to(loss, rows.shape)
    high = wide.astype(BF16).astype(F32)
    return jnp.where(rows == 0, high, jnp.where(rows == 1, wide - high, 0.0)).astype(BF16)


def tail_sum(tail, n):
    tail = tail.astype(F32)
    return tail[0:1, :n] + tail[1:2, :n]


def halves_kernel(spot, c, i2, i1, i3, b, a, i0, ih, th, raw, arrived):
    r = a.shape[0]
    sources = (a, b, c, i0, i1, i2, i3)
    copies = [
        pltpu.make_async_copy(source, raw.at[k], arrived.at[k]) for k, source in enumerate(sources)
    ]
    for copy in copies:
        copy.start()
    copies[0].wait()
    own = half_of(raw.at[0])
    th[pl.ds(0, r), :] = own
    copies[1].wait()
    th[pl.ds(r, r), :] = half_of(raw.at[1])
    copies[2].wait()

    @pl.when(spot[0] < 2)
    def _():
        th[pl.ds(2 * r, r), :] = own

    @pl.when(spot[0] >= 2)
    def _():
        th[pl.ds(2 * r, r), :] = half_of(raw.at[2])

    for k in range(4):
        copies[3 + k].wait()
        ih[pl.ds(k * r, r), :] = half_of(raw.at[3 + k])


def band(scalars, ih, th, p, diagonal):
    r = th.shape[0] // 3
    n = 2 * r
    temper, bias = scalars[0], scalars[1]
    sums, parts = [], []
    for half in range(2):
        logits = bias + temper * lax.dot_general(
            ih[pl.ds(half * n, n), :], th[pl.ds(half * r, n), :], NT, preferred_element_type=F32
        )
        margin = logits
        if diagonal and half == 0:
            rows = lax.broadcasted_iota(jnp.int32, logits.shape, 0)
            cols = lax.broadcasted_iota(jnp.int32, logits.shape, 1)
            positive = (rows == cols) & (cols < r)
            margin = jnp.where(positive, -logits, logits)
        grown = jnp.exp(margin)
        whole = 1.0 + grown
        slope = grown / whole
        losses = jnp.where(
            grown < 0.00390625,
            grown * (1.0 - grown * (0.5 - grown * (1.0 / 3.0))),
            jnp.log(whole),
        )
        if diagonal and half == 0:
            slope = jnp.where(positive, -slope, slope)
        p[pl.ds(half * n, n), :] = slope.astype(BF16)
        losses = jnp.sum(losses.reshape(n // 8, 8, n), axis=0)
        sums.append(jnp.broadcast_to(jnp.sum(losses, axis=0, keepdims=True), (8, n)))
    for half in range(2):
        parts.append(
            lax.dot_general(
                p[pl.ds(half * n, n), :], ih[pl.ds(half * n, n), :], TN, preferred_element_type=F32
            )
        )
    near, far = parts
    return (
        (near[:r], near[r:] + far[:r], far[r:]),
        (sums[0], pltpu.roll(sums[0], r, 1) + sums[1], pltpu.roll(sums[1], r, 1)),
    )


def own_pairs_kernel(scalars, ih, th, p, own, sums):
    parts, losses = band(scalars, ih, th, p, True)
    for place in range(3):
        own[place] = parts[place]
        sums[place] = losses[place]


def sibling_pairs_kernel(scalars, ih, th, after, p, send):
    del after
    parts, losses = band(scalars, ih, th, p, False)
    r, width = parts[0].shape
    for place in range(3):
        send[place, pl.ds(0, r), :] = parts[place].astype(BF16)
        send[place, pl.ds(r, TAIL), :] = jnp.zeros((TAIL, width), BF16)
        send[place, pl.ds(r, TAIL), pl.ds(0, 2 * r)] = tail_of(losses[place][:1])


def spread_kernel(p_own, p_sib, t_own, t_sib, image_own, image_1, image_2, image_3):
    r = image_own.shape[0]
    n = 2 * r
    for half, (first, second) in ((1, (image_2, image_3)), (0, (image_own, image_1))):
        total = 0.0
        for p, t in ((p_own, t_own), (p_sib, t_sib)):
            total = total + lax.dot_general(
                p[pl.ds(half * n, n), :], t[pl.ds(half * r, n), :], NN, preferred_element_type=F32
            )
        first[...] = total[:r].astype(first.dtype)
        second[...] = total[r:].astype(second.dtype)


def join_kernel(own, got, sums, after, b_back, c_back):
    del after
    r = own.shape[1]
    n = sums.shape[2]
    for place, out in ((1, b_back), (2, c_back)):
        out[pl.ds(0, r), :] = (own[place] + got[place, pl.ds(0, r), :].astype(F32)).astype(BF16)
        loss = sums[place][:1] + tail_sum(got[place, pl.ds(r, TAIL), :], n)
        out[pl.ds(r, TAIL), :] = jnp.zeros((TAIL, out.shape[1]), BF16)
        out[pl.ds(r, TAIL), pl.ds(0, n)] = tail_of(loss)


def tangent(total, ref, temper):
    unit, scale = unit_of(ref)
    total = temper * total
    return (total - unit * jnp.sum(unit * total, axis=-1, keepdims=True)) * scale


def image_end_kernel(scalars, images, own, a, b, c, grad):
    total = own[...] + a[...].astype(F32) + b[...].astype(F32) + c[...].astype(F32)
    grad[...] = tangent(total, images, scalars[0])


def text_end_kernel(scalars, spot, texts, own, got, sums, b_got, c_got, grad, loss):
    r = texts.shape[0]
    n = sums.shape[2]

    def here(place):
        rows = own[place] + got[place, pl.ds(0, r), :].astype(F32)
        return rows, sums[place][:1] + tail_sum(got[place, pl.ds(r, TAIL), :], n)

    total, losses = here(0)
    more, more_losses = here(2)
    even = spot[0] < 2
    total = total + jnp.where(even, more, 0.0)
    losses = losses + jnp.where(even, more_losses, 0.0)
    for ref in (b_got, c_got):
        total = total + ref[pl.ds(0, r), :].astype(F32)
        losses = losses + tail_sum(ref[pl.ds(r, TAIL), :], n)
    grad[...] = tangent(total, texts, scalars[0])
    loss[...] = jnp.broadcast_to(losses / (VISITS * 4 * r), loss.shape)


def call(kernel, outs, name, smem, vmem, hbm=(), scratch=()):
    return pl.pallas_call(
        kernel,
        out_shape=outs,
        in_specs=[SMEM] * len(smem) + [VMEM] * len(vmem) + [HBM] * len(hbm),
        out_specs=tuple(VMEM for _ in outs),
        scratch_shapes=scratch,
        compiler_params=PARAMS,
        name=name,
    )(*smem, *vmem, *(pltpu.with_memory_space_constraint(value, pltpu.HBM) for value in hbm))


def on_device(lines, images, texts, log_temp, bias):
    r, width = images.shape
    n = 2 * r
    shape = jax.ShapeDtypeStruct
    half, long = shape((r, width), BF16), shape((r, width), F32)

    def send(value, name, **way):
        with jax.named_scope(name):
            return moved(value, lines, **way)

    scalars = jnp.stack([jnp.exp(log_temp), bias])
    spot = lax.axis_index("img") % 2 * 2 + lax.axis_index("txt") // 2
    spot = jnp.reshape(spot, (1,)).astype(jnp.int32)
    c_own = send(texts, "texts_two_up", up=2, odd_only=True)
    b_own = send(texts, "texts_one_up", up=1)
    image_2 = send(images, "images_across", flip=2)
    image_3 = send(images, "images_beside_far", flip=3)
    image_1 = send(images, "images_beside", flip=1)
    ih, t_own = call(
        halves_kernel,
        (shape((4 * r, width), BF16), shape((3 * r, width), BF16)),
        "halves",
        [spot],
        [],
        [c_own, image_2, image_1, image_3, b_own, texts, images],
        scratch=(pltpu.VMEM((7, r, width), BF16), pltpu.SemaphoreType.DMA((7,))),
    )
    t_sib = send(t_own, "texts_sibling", other=1)
    slopes = shape((4 * r, n), BF16)
    p_own, own, sums = call(
        own_pairs_kernel,
        (slopes, shape((3, r, width), F32), shape((3, 8, n), F32)),
        "own_pairs",
        [scalars],
        [ih, t_own],
    )
    p_sib, text_send = call(
        sibling_pairs_kernel,
        (slopes, shape((3, r + TAIL, width), BF16)),
        "sibling_pairs",
        [scalars],
        [ih, t_sib, sums],
    )
    got = send(text_send, "text_parts_sibling", other=1)
    image_own, out_1, out_2, out_3 = call(
        spread_kernel, (long, half, half, half), "spread", [], [p_own, p_sib, t_own, t_sib]
    )
    back_2 = send(out_2, "image_parts_across", flip=2)
    back_3 = send(out_3, "image_parts_beside_far", flip=3)
    back_1 = send(out_1, "image_parts_beside", flip=1)
    back = shape((r + TAIL, width), BF16)
    b_back, c_back = call(join_kernel, (back, back), "join", [], [own, got, sums, out_2])
    c_got = send(c_back, "text_parts_two_down", up=-2, odd_only=True)
    b_got = send(b_back, "text_parts_one_down", up=-1)
    (image_grad,) = call(
        image_end_kernel, (long,), "image_end", [scalars], [images, image_own, back_1, back_2, back_3]
    )
    text_grad, loss = call(
        text_end_kernel,
        (long, shape((8, n), F32)),
        "text_end",
        [scalars, spot],
        [texts, own, got, sums, b_got, c_got],
    )
    return loss[0, :r], image_grad, text_grad


def solution(mesh):
    from jax.sharding import PartitionSpec as P

    lines = mesh.shape["img"] // 2
    rows = P(AXES, None)
    return jax.shard_map(
        functools.partial(on_device, lines),
        mesh=mesh,
        in_specs=(rows, rows, P(), P()),
        out_specs=(P(AXES), rows, rows),
        check_vma=False,
    )
```

```python
import functools

import jax
import jax.numpy as jnp
from jax import lax
from jax.experimental import pallas as pl
from jax.experimental.pallas import tpu as pltpu

EPSILON = 1e-06
VISITS = 4
TAIL = 16
AXES = ("img", "txt")
F32, BF16 = jnp.float32, jnp.bfloat16
NT = (((1,), (1,)), ((), ()))
NN = (((1,), (0,)), ((), ()))
TN = (((0,), (0,)), ((), ()))
HBM = pl.BlockSpec(memory_space=pltpu.HBM)
VMEM = pl.BlockSpec(memory_space=pltpu.VMEM)
SMEM = pl.BlockSpec(memory_space=pltpu.SMEM)
PARAMS = pltpu.CompilerParams(vmem_limit_bytes=48 * 1024 * 1024)


def moved(value, lines, up=0, flip=0, other=0, odd_only=False):
    route = []
    for line in range(lines):
        for x in range(4):
            if odd_only and x < 2:
                continue
            for c in range(2):
                here = line * 8 + x * 2 + c
                there = (line + up) % lines * 8 + (x ^ flip) * 2 + (c ^ other)
                route.append((here, there))
    return lax.ppermute(value, AXES, route)


def unit_of(ref):
    wide = ref[...].astype(F32)
    square = jnp.sum(wide * wide, axis=-1, keepdims=True) + EPSILON
    scale = 1.0 / jnp.sqrt(square)
    return wide * scale, scale


def half_of(ref):
    return unit_of(ref)[0].astype(BF16)


def tail_of(loss):
    rows = lax.broadcasted_iota(jnp.int32, (TAIL, loss.shape[1]), 0)
    wide = jnp.broadcast_to(loss, rows.shape)
    high = wide.astype(BF16).astype(F32)
    return jnp.where(rows == 0, high, jnp.where(rows == 1, wide - high, 0.0)).astype(BF16)


def tail_sum(tail, n):
    tail = tail.astype(F32)
    return tail[0:1, :n] + tail[1:2, :n]


def halves_kernel(b, a, i2, i1, i3, i0, ih, ah, bh, raw, arrived):
    r = i0.shape[0]
    places = ((b, bh, 0), (a, ah, 0), (i0, ih, 0), (i2, ih, 2), (i1, ih, 1), (i3, ih, 3))
    copies, at = [], 0
    for k, (ref, _, _) in enumerate(places):
        rows = ref.shape[0]
        copies.append(pltpu.make_async_copy(ref, raw.at[pl.ds(at, rows), :], arrived.at[k]))
        copies[-1].start()
        at += rows
    at = 0
    for copy, (ref, out, place) in zip(copies, places):
        rows = ref.shape[0]
        copy.wait()
        out[pl.ds(place * r, rows), :] = half_of(raw.at[pl.ds(at, rows), :])
        at += rows


def late_halves_kernel(after, c, out):
    del after
    out[...] = half_of(c)


def temper_of(log_temp, lanes):
    return jnp.exp(jnp.full((1, lanes), log_temp[0], F32))


def tile(log_temp, bias, images, texts, diagonal=False):
    rows, cols = images.shape[0], texts.shape[0]
    logits = bias[0] + temper_of(log_temp, cols) * dot(images, texts, NT)
    margin = logits
    if diagonal:
        row = lax.broadcasted_iota(jnp.int32, logits.shape, 0)
        col = lax.broadcasted_iota(jnp.int32, logits.shape, 1)
        positive = (row == col) & (col < cols // 2)
        margin = jnp.where(positive, -logits, logits)
    grown = jnp.exp(margin)
    whole = 1.0 + grown
    inverse = pl.reciprocal(whole, approx=True)
    inverse = inverse * (2.0 - whole * inverse)
    slope = grown * inverse
    left = (grown - (whole - 1.0)) * inverse
    if diagonal:
        slope = jnp.where(positive, -slope, slope)
    q = rows // 4
    product = (whole[:q] * whole[q : 2 * q]) * (whole[2 * q : 3 * q] * whole[3 * q :])
    left = (left[:q] + left[q : 2 * q]) + (left[2 * q : 3 * q] + left[3 * q :])
    losses = jnp.sum((jnp.log(product) + left).reshape(q // 8, 8, cols), axis=0)
    return slope.astype(BF16), jnp.sum(losses, axis=0, keepdims=True)


def halved(sums, r):
    sums = jnp.broadcast_to(sums, (8, 2 * r))
    return sums[:1, :r], pltpu.roll(sums, r, 1)[:1, :r]


def dot(left, right, dims):
    return lax.dot_general(left, right, dims, preferred_element_type=F32)


def band(log_temp, bias, spot, ih, th, near, far, extra, part, losses, diagonal):
    r = th.shape[0] // 2
    n = 2 * r
    slope, sums = tile(log_temp, bias, ih[:n], th[...], diagonal)
    near[...] = slope
    sums_a, sums_b = halved(sums, r)
    slope, sums = tile(log_temp, bias, ih[n:], th[r:])
    far[...] = slope
    losses[1] = jnp.broadcast_to(sums_b + sums, losses.shape[1:])
    losses[0] = jnp.broadcast_to(sums_a, losses.shape[1:])
    extra[...] = jnp.zeros_like(extra)
    both = dot(near[...], ih[:n], TN)
    part[0] = both[:r]
    part[1] = both[r:] + dot(far[...], ih[n:], TN)

    @pl.when(spot[0] < 2)
    def _():
        slope, sums = tile(log_temp, bias, ih[n:], th[:r])
        extra[...] = slope
        losses[0] += jnp.broadcast_to(sums, losses.shape[1:])
        part[0] += dot(extra[...], ih[n:], TN)


def put_rows(out, rows):
    out[pl.ds(0, rows.shape[0]), :] = rows.astype(BF16)
    out[pl.ds(rows.shape[0], TAIL), :] = jnp.zeros((TAIL, rows.shape[1]), BF16)


def put_send(send, place, part, sums):
    r, width = part.shape
    send[place, pl.ds(0, r), :] = part.astype(BF16)
    send[place, pl.ds(r, TAIL), :] = jnp.zeros((TAIL, width), BF16)
    send[place, pl.ds(r, TAIL), pl.ds(0, r)] = tail_of(sums)


def own_pairs_kernel(log_temp, bias, spot, ih, a, b, near, far, extra, part, losses, th):
    r = th.shape[0] // 2
    th[pl.ds(0, r), :] = of_core(a, spot[1])
    th[pl.ds(r, r), :] = of_core(b, spot[1])
    band(log_temp, bias, spot, ih, th, near, far, extra, part, losses, True)


def of_core(ref, core):
    r = ref.shape[0] // 2
    return ref[pl.ds(pl.multiple_of(core * r, r), r), :]


def sibling_pairs_kernel(log_temp, bias, spot, ih, a, b, after, near, far, extra, send, th, part, losses):
    del after
    r = th.shape[0] // 2
    th[pl.ds(0, r), :] = of_core(a, 1 - spot[1])
    th[pl.ds(r, r), :] = of_core(b, 1 - spot[1])
    band(log_temp, bias, spot, ih, th, near, far, extra, part, losses, False)
    for place in range(2):
        put_send(send, place, part[place], losses[place][:1])


def spread_kernel(
    spot, near_o, far_o, extra_o, a, b, near_s, far_s, extra_s, image_own, image_1, rest, t_o, t_s
):
    r = image_own.shape[0]
    for core, th in ((spot[1], t_o), (1 - spot[1], t_s)):
        th[pl.ds(0, r), :] = of_core(a, core)
        th[pl.ds(r, r), :] = of_core(b, core)
    rest[...] = dot(far_o[...], t_o[r:], NN) + dot(far_s[...], t_s[r:], NN)

    @pl.when(spot[0] < 2)
    def _():
        rest[...] += dot(extra_o[...], t_o[:r], NN) + dot(extra_s[...], t_s[:r], NN)

    total = dot(near_o[...], t_o[...], NN) + dot(near_s[...], t_s[...], NN)
    image_own[...] = total[:r]
    put_rows(image_1, total[r:])


def late_pairs_kernel(log_temp, bias, spot, ih, c, rest, image_2, image_3, own, sums, send, texts, slopes):
    r = own.shape[0]
    n = 2 * r

    @pl.when(spot[0] >= 2)
    def _():
        texts[pl.ds(0, r), :] = of_core(c, spot[1])
        texts[pl.ds(r, r), :] = of_core(c, 1 - spot[1])
        slope, losses = tile(log_temp, bias, ih[n:], texts[...])
        slopes[...] = slope
        both = dot(slopes[...], ih[n:], TN)
        sums_own, sums_sibling = halved(losses, r)
        own[...] = both[:r]
        sums[...] = jnp.broadcast_to(sums_own, sums.shape)
        put_send(send, 0, both[r:], sums_sibling)
        total = rest[...] + dot(slopes[...], texts[...], NN)
        put_rows(image_2, total[:r])
        put_rows(image_3, total[r:])

    @pl.when(spot[0] < 2)
    def _():
        own[...] = jnp.zeros_like(own)
        sums[...] = jnp.zeros_like(sums)
        send[...] = jnp.zeros_like(send)
        put_rows(image_2, rest[:r])
        put_rows(image_3, rest[r:])


def joined(part, sums, got):
    r = part.shape[0]
    return part + got[:r].astype(F32), sums + tail_sum(got[r:], r)


def join_kernel(part, losses, got, late_part, late_sums, late_got, b_back, c_back):
    put_send(b_back, 0, *joined(part[1], losses[1][:1], got[1]))
    put_send(c_back, 0, *joined(late_part[...], late_sums[:1], late_got[0]))


def tangent(total, ref, log_temp):
    unit, scale = unit_of(ref)
    total = temper_of(log_temp, ref.shape[1]) * total
    return (total - unit * jnp.sum(unit * total, axis=-1, keepdims=True)) * scale


def image_end_kernel(log_temp, images, own, a, b, c, grad):
    r = own.shape[0]
    total = own[...] + a[:r].astype(F32) + b[:r].astype(F32) + c[:r].astype(F32)
    grad[...] = tangent(total, images, log_temp)


def text_end_kernel(log_temp, texts, part, losses, got, c_got, b_got, grad, loss):
    r = texts.shape[0]
    total, sums = joined(part[0], losses[0][:1], got[0])
    for ref in (c_got, b_got):
        total, sums = joined(total, sums, ref[0])
    grad[...] = tangent(total, texts, log_temp)
    loss[...] = sums / (VISITS * 4 * r)


def call(kernel, outs, name, smem, vmem, hbm=(), scratch=()):
    return pl.pallas_call(
        kernel,
        out_shape=outs,
        in_specs=[SMEM] * len(smem) + [VMEM] * len(vmem) + [HBM] * len(hbm),
        out_specs=tuple(VMEM for _ in outs),
        scratch_shapes=scratch,
        compiler_params=PARAMS,
        name=name,
    )(*smem, *vmem, *(pltpu.with_memory_space_constraint(value, pltpu.HBM) for value in hbm))


def on_device(lines, images, texts, log_temp, bias):
    r, width = images.shape
    n = 2 * r
    shape = jax.ShapeDtypeStruct
    half, long = shape((r, width), BF16), shape((r, width), F32)
    loss_rows = shape((2, 8, r), F32)
    wide = shape((r + TAIL, width), BF16)

    def send(value, name, **way):
        with jax.named_scope(name):
            return moved(value, lines, **way)

    log_temp, bias = jnp.reshape(log_temp, (1,)), jnp.reshape(bias, (1,))
    txt = lax.axis_index("txt")
    spot = jnp.stack([lax.axis_index("img") % 2 * 2 + txt // 2, txt % 2]).astype(jnp.int32)
    pairs = [[2 * k, 2 * k + 1] for k in range(4 * lines)]

    def of_both(value, name):
        with jax.named_scope(name):
            return lax.all_gather(value, AXES, axis_index_groups=pairs, axis=0, tiled=True)

    b_own = send(texts, "texts_one_up", up=1)
    c_raw = send(texts, "texts_two_up", up=2, odd_only=True)
    image_2 = send(images, "images_across", flip=2)
    image_1 = send(images, "images_beside", flip=1)
    image_3 = send(images, "images_beside_far", flip=3)
    a_raw = of_both(texts, "texts_of_both_cores")
    b_raw = of_both(b_own, "moved_texts_of_both_cores")
    ih, a_both, b_both = call(
        halves_kernel,
        (shape((4 * r, width), BF16), shape((n, width), BF16), shape((n, width), BF16)),
        "halves",
        [],
        [],
        [b_raw, a_raw, image_2, image_1, image_3, images],
        scratch=(pltpu.VMEM((8 * r, width), BF16), pltpu.SemaphoreType.DMA((6,))),
    )
    slopes = (shape((n, n), BF16), shape((n, r), BF16), shape((n, r), BF16))
    pair = pltpu.VMEM((n, width), BF16)
    near_o, far_o, extra_o, part, losses = call(
        own_pairs_kernel,
        (*slopes, shape((2, r, width), F32), loss_rows),
        "own_pairs",
        [log_temp, bias, spot],
        [ih, a_both, b_both],
        scratch=(pair,),
    )
    near_s, far_s, extra_s, text_send = call(
        sibling_pairs_kernel,
        (*slopes, shape((2, r + TAIL, width), BF16)),
        "sibling_pairs",
        [log_temp, bias, spot],
        [ih, a_both, b_both, losses],
        scratch=(pair, pltpu.VMEM((2, r, width), F32), pltpu.VMEM((2, 8, r), F32)),
    )
    (c_own,) = call(late_halves_kernel, (half,), "late_halves", [], [extra_s, c_raw])
    c_both = of_both(c_own, "late_texts_of_both_cores")
    got = send(text_send, "text_parts_sibling", other=1)
    image_own, out_1, rest = call(
        spread_kernel,
        (long, wide, shape((n, width), F32)),
        "spread",
        [spot],
        [near_o, far_o, extra_o, a_both, b_both, near_s, far_s, extra_s],
        scratch=(pair, pair),
    )
    back = shape((1, r + TAIL, width), BF16)
    out_2, out_3, late_part, late_sums, late_send = call(
        late_pairs_kernel,
        (wide, wide, long, shape((8, r), F32), back),
        "late_pairs",
        [log_temp, bias, spot],
        [ih, c_both, rest],
        scratch=(pltpu.VMEM((n, width), BF16), pltpu.VMEM((n, n), BF16)),
    )
    late_got = send(late_send, "late_text_parts_sibling", other=1)
    back_2 = send(out_2, "image_parts_across", flip=2)
    back_3 = send(out_3, "image_parts_beside_far", flip=3)
    back_1 = send(out_1, "image_parts_beside", flip=1)
    b_back, c_back = call(
        join_kernel, (back, back), "join", [], [part, losses, got, late_part, late_sums, late_got]
    )
    c_got = send(c_back, "text_parts_two_down", up=-2, odd_only=True)
    b_got = send(b_back, "text_parts_one_down", up=-1)
    (image_grad,) = call(
        image_end_kernel, (long,), "image_end", [log_temp], [images, image_own, back_1, back_2, back_3]
    )
    text_grad, loss = call(
        text_end_kernel,
        (long, shape((1, r), F32)),
        "text_end",
        [log_temp],
        [texts, part, losses, got, c_got, b_got],
    )
    return jnp.reshape(loss, (r,)), image_grad, text_grad


def solution(mesh):
    from jax.sharding import PartitionSpec as P

    lines = mesh.shape["img"] // 2
    rows = P(AXES, None)
    return jax.shard_map(
        functools.partial(on_device, lines),
        mesh=mesh,
        in_specs=(rows, rows, P(), P()),
        out_specs=(P(AXES), rows, rows),
        check_vma=False,
    )
```

```python
import functools

import jax
import jax.numpy as jnp
from jax import lax
from jax.experimental import pallas as pl
from jax.experimental.pallas import tpu as pltpu

EPSILON = 1e-06
VISITS = 4
PLANES = 12
TAIL = 16
AXES = ("img", "txt")
F32, BF16 = jnp.float32, jnp.bfloat16
NT = (((1,), (1,)), ((), ()))
NN = (((1,), (0,)), ((), ()))
TN = (((0,), (0,)), ((), ()))
HBM = pl.BlockSpec(memory_space=pltpu.HBM)
VMEM = pl.BlockSpec(memory_space=pltpu.VMEM)
SMEM = pl.BlockSpec(memory_space=pltpu.SMEM)
PARAMS = pltpu.CompilerParams(vmem_limit_bytes=48 * 1024 * 1024)


def moved(value, lines, up=0, flip=0, other=0, odd_only=False, round_end=None):
    route = []
    for line in range(lines):
        if round_end is not None and round_end != (line % PLANES + up < 0):
            continue
        for x in range(4):
            if odd_only and x < 2:
                continue
            for c in range(2):
                here = line * 8 + x * 2 + c
                there = (line + up) % lines * 8 + (x ^ flip) * 2 + (c ^ other)
                route.append((here, there))
    return lax.ppermute(value, AXES, route)


def unit_of(ref):
    wide = ref[...].astype(F32)
    square = jnp.sum(wide * wide, axis=-1, keepdims=True) + EPSILON
    scale = 1.0 / jnp.sqrt(square)
    return wide * scale, scale


def half_of(ref):
    return unit_of(ref)[0].astype(BF16)


def tail_of(loss):
    rows = lax.broadcasted_iota(jnp.int32, (TAIL, loss.shape[1]), 0)
    wide = jnp.broadcast_to(loss, rows.shape)
    high = wide.astype(BF16).astype(F32)
    return jnp.where(rows == 0, high, jnp.where(rows == 1, wide - high, 0.0)).astype(BF16)


def tail_sum(tail, n):
    tail = tail.astype(F32)
    return tail[0:1, :n] + tail[1:2, :n]


def halves_kernel(b, a, i2, i1, i3, i0, ih, ah, bh, raw, arrived):
    r = i0.shape[0]
    places = ((b, bh, 0), (a, ah, 0), (i0, ih, 0), (i2, ih, 2), (i1, ih, 1), (i3, ih, 3))
    copies, at = [], 0
    for k, (ref, _, _) in enumerate(places):
        rows = ref.shape[0]
        copies.append(pltpu.make_async_copy(ref, raw.at[pl.ds(at, rows), :], arrived.at[k]))
        copies[-1].start()
        at += rows
    at = 0
    for copy, (ref, out, place) in zip(copies, places):
        rows = ref.shape[0]
        copy.wait()
        out[pl.ds(place * r, rows), :] = half_of(raw.at[pl.ds(at, rows), :])
        at += rows


def late_halves_kernel(after, c, out):
    del after
    out[...] = half_of(c)


def temper_of(log_temp, lanes):
    return jnp.exp(jnp.full((1, lanes), log_temp[0], F32))


def tile(log_temp, bias, images, texts, diagonal=False):
    rows, cols = images.shape[0], texts.shape[0]
    logits = bias[0] + temper_of(log_temp, cols) * dot(images, texts, NT)
    margin = logits
    if diagonal:
        row = lax.broadcasted_iota(jnp.int32, logits.shape, 0)
        col = lax.broadcasted_iota(jnp.int32, logits.shape, 1)
        positive = (row == col) & (col < cols // 2)
        margin = jnp.where(positive, -logits, logits)
    grown = jnp.exp(margin)
    whole = 1.0 + grown
    inverse = pl.reciprocal(whole, approx=True)
    inverse = inverse * (2.0 - whole * inverse)
    slope = grown * inverse
    left = (grown - (whole - 1.0)) * inverse
    if diagonal:
        slope = jnp.where(positive, -slope, slope)
    q = rows // 4
    product = (whole[:q] * whole[q : 2 * q]) * (whole[2 * q : 3 * q] * whole[3 * q :])
    left = (left[:q] + left[q : 2 * q]) + (left[2 * q : 3 * q] + left[3 * q :])
    losses = jnp.sum((jnp.log(product) + left).reshape(q // 8, 8, cols), axis=0)
    return slope.astype(BF16), jnp.sum(losses, axis=0, keepdims=True)


def halved(sums, r):
    sums = jnp.broadcast_to(sums, (8, 2 * r))
    return sums[:1, :r], pltpu.roll(sums, r, 1)[:1, :r]


def dot(left, right, dims):
    return lax.dot_general(left, right, dims, preferred_element_type=F32)


def band(log_temp, bias, spot, ih, th, near, far, extra, part, losses, diagonal):
    r = th.shape[0] // 2
    n = 2 * r
    slope, sums = tile(log_temp, bias, ih[:n], th[...], diagonal)
    near[...] = slope
    sums_a, sums_b = halved(sums, r)
    slope, sums = tile(log_temp, bias, ih[n:], th[r:])
    far[...] = slope
    losses[1] = jnp.broadcast_to(sums_b + sums, losses.shape[1:])
    losses[0] = jnp.broadcast_to(sums_a, losses.shape[1:])
    extra[...] = jnp.zeros_like(extra)
    both = dot(near[...], ih[:n], TN)
    part[0] = both[:r]
    part[1] = both[r:] + dot(far[...], ih[n:], TN)

    @pl.when(spot[0] < 2)
    def _():
        slope, sums = tile(log_temp, bias, ih[n:], th[:r])
        extra[...] = slope
        losses[0] += jnp.broadcast_to(sums, losses.shape[1:])
        part[0] += dot(extra[...], ih[n:], TN)


def put_rows(out, rows):
    out[pl.ds(0, rows.shape[0]), :] = rows.astype(BF16)
    out[pl.ds(rows.shape[0], TAIL), :] = jnp.zeros((TAIL, rows.shape[1]), BF16)


def put_send(send, place, part, sums):
    r, width = part.shape
    send[place, pl.ds(0, r), :] = part.astype(BF16)
    send[place, pl.ds(r, TAIL), :] = jnp.zeros((TAIL, width), BF16)
    send[place, pl.ds(r, TAIL), pl.ds(0, r)] = tail_of(sums)


def own_pairs_kernel(log_temp, bias, spot, ih, a, b, near, far, extra, part, losses, th):
    r = th.shape[0] // 2
    th[pl.ds(0, r), :] = of_core(a, spot[1])
    th[pl.ds(r, r), :] = of_core(b, spot[1])
    band(log_temp, bias, spot, ih, th, near, far, extra, part, losses, True)


def of_core(ref, core):
    r = ref.shape[0] // 2
    return ref[pl.ds(pl.multiple_of(core * r, r), r), :]


def sibling_pairs_kernel(log_temp, bias, spot, ih, a, b, after, near, far, extra, send, th, part, losses):
    del after
    r = th.shape[0] // 2
    th[pl.ds(0, r), :] = of_core(a, 1 - spot[1])
    th[pl.ds(r, r), :] = of_core(b, 1 - spot[1])
    band(log_temp, bias, spot, ih, th, near, far, extra, part, losses, False)
    for place in range(2):
        put_send(send, place, part[place], losses[place][:1])


def spread_kernel(
    spot, near_o, far_o, extra_o, a, b, near_s, far_s, extra_s, image_own, image_1, rest, t_o, t_s
):
    r = image_own.shape[0]
    for core, th in ((spot[1], t_o), (1 - spot[1], t_s)):
        th[pl.ds(0, r), :] = of_core(a, core)
        th[pl.ds(r, r), :] = of_core(b, core)
    rest[...] = dot(far_o[...], t_o[r:], NN) + dot(far_s[...], t_s[r:], NN)

    @pl.when(spot[0] < 2)
    def _():
        rest[...] += dot(extra_o[...], t_o[:r], NN) + dot(extra_s[...], t_s[:r], NN)

    total = dot(near_o[...], t_o[...], NN) + dot(near_s[...], t_s[...], NN)
    image_own[...] = total[:r]
    put_rows(image_1, total[r:])


def late_pairs_kernel(log_temp, bias, spot, ih, c, rest, image_2, image_3, own, sums, send, texts, slopes):
    r = own.shape[0]
    n = 2 * r

    @pl.when(spot[0] >= 2)
    def _():
        texts[pl.ds(0, r), :] = of_core(c, spot[1])
        texts[pl.ds(r, r), :] = of_core(c, 1 - spot[1])
        slope, losses = tile(log_temp, bias, ih[n:], texts[...])
        slopes[...] = slope
        both = dot(slopes[...], ih[n:], TN)
        sums_own, sums_sibling = halved(losses, r)
        own[...] = both[:r]
        sums[...] = jnp.broadcast_to(sums_own, sums.shape)
        put_send(send, 0, both[r:], sums_sibling)
        total = rest[...] + dot(slopes[...], texts[...], NN)
        put_rows(image_2, total[:r])
        put_rows(image_3, total[r:])

    @pl.when(spot[0] < 2)
    def _():
        own[...] = jnp.zeros_like(own)
        sums[...] = jnp.zeros_like(sums)
        send[...] = jnp.zeros_like(send)
        put_rows(image_2, rest[:r])
        put_rows(image_3, rest[r:])


def joined(part, sums, got):
    r = part.shape[0]
    return part + got[:r].astype(F32), sums + tail_sum(got[r:], r)


def join_kernel(part, losses, got, late_part, late_sums, late_got, b_back, c_back):
    put_send(b_back, 0, *joined(part[1], losses[1][:1], got[1]))
    put_send(c_back, 0, *joined(late_part[...], late_sums[:1], late_got[0]))


def tangent(total, ref, log_temp):
    unit, scale = unit_of(ref)
    total = temper_of(log_temp, ref.shape[1]) * total
    return (total - unit * jnp.sum(unit * total, axis=-1, keepdims=True)) * scale


def image_end_kernel(log_temp, images, own, a, b, c, grad):
    r = own.shape[0]
    total = own[...] + a[:r].astype(F32) + b[:r].astype(F32) + c[:r].astype(F32)
    grad[...] = tangent(total, images, log_temp)


def text_end_kernel(log_temp, texts, part, losses, got, c_end, b_got, b_end, c_got, grad, loss):
    r = texts.shape[0]
    total, sums = joined(part[0], losses[0][:1], got[0])
    for ref in (c_end, b_got, b_end, c_got):
        total, sums = joined(total, sums, ref[0])
    grad[...] = tangent(total, texts, log_temp)
    loss[...] = sums / (VISITS * 4 * r)


def call(kernel, outs, name, smem, vmem, hbm=(), scratch=()):
    return pl.pallas_call(
        kernel,
        out_shape=outs,
        in_specs=[SMEM] * len(smem) + [VMEM] * len(vmem) + [HBM] * len(hbm),
        out_specs=tuple(VMEM for _ in outs),
        scratch_shapes=scratch,
        compiler_params=PARAMS,
        name=name,
    )(*smem, *vmem, *(pltpu.with_memory_space_constraint(value, pltpu.HBM) for value in hbm))


def on_device(lines, images, texts, log_temp, bias):
    r, width = images.shape
    n = 2 * r
    shape = jax.ShapeDtypeStruct
    half, long = shape((r, width), BF16), shape((r, width), F32)
    loss_rows = shape((2, 8, r), F32)
    wide = shape((r + TAIL, width), BF16)

    def send(value, name, **way):
        with jax.named_scope(name):
            return moved(value, lines, **way)

    log_temp, bias = jnp.reshape(log_temp, (1,)), jnp.reshape(bias, (1,))
    txt = lax.axis_index("txt")
    spot = jnp.stack([lax.axis_index("img") % 2 * 2 + txt // 2, txt % 2]).astype(jnp.int32)
    pairs = [[2 * k, 2 * k + 1] for k in range(4 * lines)]

    def of_both(value, name):
        with jax.named_scope(name):
            return lax.all_gather(value, AXES, axis_index_groups=pairs, axis=0, tiled=True)

    b_own = send(texts, "texts_one_up", up=1)
    c_raw = send(texts, "texts_two_up", up=2, odd_only=True)
    image_2 = send(images, "images_across", flip=2)
    image_1 = send(images, "images_beside", flip=1)
    image_3 = send(images, "images_beside_far", flip=3)
    a_raw = of_both(texts, "texts_of_both_cores")
    b_raw = of_both(b_own, "moved_texts_of_both_cores")
    ih, a_both, b_both = call(
        halves_kernel,
        (shape((4 * r, width), BF16), shape((n, width), BF16), shape((n, width), BF16)),
        "halves",
        [],
        [],
        [b_raw, a_raw, image_2, image_1, image_3, images],
        scratch=(pltpu.VMEM((8 * r, width), BF16), pltpu.SemaphoreType.DMA((6,))),
    )
    slopes = (shape((n, n), BF16), shape((n, r), BF16), shape((n, r), BF16))
    pair = pltpu.VMEM((n, width), BF16)
    near_o, far_o, extra_o, part, losses = call(
        own_pairs_kernel,
        (*slopes, shape((2, r, width), F32), loss_rows),
        "own_pairs",
        [log_temp, bias, spot],
        [ih, a_both, b_both],
        scratch=(pair,),
    )
    near_s, far_s, extra_s, text_send = call(
        sibling_pairs_kernel,
        (*slopes, shape((2, r + TAIL, width), BF16)),
        "sibling_pairs",
        [log_temp, bias, spot],
        [ih, a_both, b_both, losses],
        scratch=(pair, pltpu.VMEM((2, r, width), F32), pltpu.VMEM((2, 8, r), F32)),
    )
    (c_own,) = call(late_halves_kernel, (half,), "late_halves", [], [extra_s, c_raw])
    c_both = of_both(c_own, "late_texts_of_both_cores")
    got = send(text_send, "text_parts_sibling", other=1)
    image_own, out_1, rest = call(
        spread_kernel,
        (long, wide, shape((n, width), F32)),
        "spread",
        [spot],
        [near_o, far_o, extra_o, a_both, b_both, near_s, far_s, extra_s],
        scratch=(pair, pair),
    )
    back = shape((1, r + TAIL, width), BF16)
    out_2, out_3, late_part, late_sums, late_send = call(
        late_pairs_kernel,
        (wide, wide, long, shape((8, r), F32), back),
        "late_pairs",
        [log_temp, bias, spot],
        [ih, c_both, rest],
        scratch=(pltpu.VMEM((n, width), BF16), pltpu.VMEM((n, n), BF16)),
    )
    late_got = send(late_send, "late_text_parts_sibling", other=1)
    back_2 = send(out_2, "image_parts_across", flip=2)
    back_3 = send(out_3, "image_parts_beside_far", flip=3)
    back_1 = send(out_1, "image_parts_beside", flip=1)
    b_back, c_back = call(
        join_kernel, (back, back), "join", [], [part, losses, got, late_part, late_sums, late_got]
    )
    c_got = send(c_back, "text_parts_two_down", up=-2, odd_only=True, round_end=False)
    c_end = send(c_back, "end_text_parts_two_down", up=-2, odd_only=True, round_end=True)
    b_got = send(b_back, "text_parts_one_down", up=-1, round_end=False)
    b_end = send(b_back, "end_text_parts_one_down", up=-1, round_end=True)
    (image_grad,) = call(
        image_end_kernel, (long,), "image_end", [log_temp], [images, image_own, back_1, back_2, back_3]
    )
    text_grad, loss = call(
        text_end_kernel,
        (long, shape((1, r), F32)),
        "text_end",
        [log_temp],
        [texts, part, losses, got, c_end, b_got, b_end, c_got],
    )
    return jnp.reshape(loss, (r,)), image_grad, text_grad


def solution(mesh):
    from jax.sharding import PartitionSpec as P

    lines = mesh.shape["img"] // 2
    rows = P(AXES, None)
    return jax.shard_map(
        functools.partial(on_device, lines),
        mesh=mesh,
        in_specs=(rows, rows, P(), P()),
        out_specs=(P(AXES), rows, rows),
        check_vma=False,
    )
```

```python
import functools

import jax
import jax.numpy as jnp
from jax import lax
from jax.experimental import pallas as pl
from jax.experimental.pallas import tpu as pltpu

EPSILON = 1e-06
VISITS = 4
TAIL = 16
AXES = ("img", "txt")
F32, BF16 = jnp.float32, jnp.bfloat16
NT = (((1,), (1,)), ((), ()))
NN = (((1,), (0,)), ((), ()))
TN = (((0,), (0,)), ((), ()))
HBM = pl.BlockSpec(memory_space=pltpu.HBM)
VMEM = pl.BlockSpec(memory_space=pltpu.VMEM)
SMEM = pl.BlockSpec(memory_space=pltpu.SMEM)
PARAMS = pltpu.CompilerParams(vmem_limit_bytes=48 * 1024 * 1024)


def moved(value, lines, up=0, flip=0, other=0, odd_only=False):
    route = []
    for line in range(lines):
        for x in range(4):
            if odd_only and x < 2:
                continue
            for c in range(2):
                here = line * 8 + x * 2 + c
                there = (line + up) % lines * 8 + (x ^ flip) * 2 + (c ^ other)
                route.append((here, there))
    return lax.ppermute(value, AXES, route)


def unit_of(ref):
    wide = ref[...].astype(F32)
    square = jnp.sum(wide * wide, axis=-1, keepdims=True) + EPSILON
    scale = 1.0 / jnp.sqrt(square)
    return wide * scale, scale


def half_of(ref):
    return unit_of(ref)[0].astype(BF16)


def tail_of(loss):
    rows = lax.broadcasted_iota(jnp.int32, (TAIL, loss.shape[1]), 0)
    wide = jnp.broadcast_to(loss, rows.shape)
    high = wide.astype(BF16).astype(F32)
    return jnp.where(rows == 0, high, jnp.where(rows == 1, wide - high, 0.0)).astype(BF16)


def tail_sum(tail, n):
    tail = tail.astype(F32)
    return tail[0:1, :n] + tail[1:2, :n]


def halves_kernel(spot, c, i2, i1, i3, b, a, i0, ih, th, raw, arrived):
    r = a.shape[0]
    sources = (a, b, c, i0, i1, i2, i3)
    copies = [
        pltpu.make_async_copy(source, raw.at[k], arrived.at[k]) for k, source in enumerate(sources)
    ]
    for copy in copies:
        copy.start()
    copies[0].wait()
    own = half_of(raw.at[0])
    th[pl.ds(0, r), :] = own
    copies[1].wait()
    th[pl.ds(r, r), :] = half_of(raw.at[1])
    copies[2].wait()

    @pl.when(spot[0] < 2)
    def _():
        th[pl.ds(2 * r, r), :] = own

    @pl.when(spot[0] >= 2)
    def _():
        th[pl.ds(2 * r, r), :] = half_of(raw.at[2])

    for k in range(4):
        copies[3 + k].wait()
        ih[pl.ds(k * r, r), :] = half_of(raw.at[3 + k])


def temper_of(log_temp, lanes):
    return jnp.exp(jnp.full((1, lanes), log_temp[0], F32))


def band(log_temp, bias, ih, th, p, diagonal):
    r = th.shape[0] // 3
    n = 2 * r
    temper = temper_of(log_temp, n)
    sums, parts = [], []
    for half in range(2):
        logits = bias[0] + temper * lax.dot_general(
            ih[pl.ds(half * n, n), :], th[pl.ds(half * r, n), :], NT, preferred_element_type=F32
        )
        margin = logits
        if diagonal and half == 0:
            rows = lax.broadcasted_iota(jnp.int32, logits.shape, 0)
            cols = lax.broadcasted_iota(jnp.int32, logits.shape, 1)
            positive = (rows == cols) & (cols < r)
            margin = jnp.where(positive, -logits, logits)
        grown = jnp.exp(margin)
        whole = 1.0 + grown
        inverse = pl.reciprocal(whole, approx=True)
        inverse = inverse * (2.0 - whole * inverse)
        slope = grown * inverse
        left = (grown - (whole - 1.0)) * inverse
        if diagonal and half == 0:
            slope = jnp.where(positive, -slope, slope)
        p[pl.ds(half * n, n), :] = slope.astype(BF16)
        q = n // 4
        product = (whole[:q] * whole[q : 2 * q]) * (whole[2 * q : 3 * q] * whole[3 * q :])
        left = (left[:q] + left[q : 2 * q]) + (left[2 * q : 3 * q] + left[3 * q :])
        losses = jnp.sum((jnp.log(product) + left).reshape(q // 8, 8, n), axis=0)
        sums.append(jnp.broadcast_to(jnp.sum(losses, axis=0, keepdims=True), (8, n)))
    for half in range(2):
        parts.append(
            lax.dot_general(
                p[pl.ds(half * n, n), :], ih[pl.ds(half * n, n), :], TN, preferred_element_type=F32
            )
        )
    near, far = parts
    return (
        (near[:r], near[r:] + far[:r], far[r:]),
        (sums[0], pltpu.roll(sums[0], r, 1) + sums[1], pltpu.roll(sums[1], r, 1)),
    )


def own_pairs_kernel(log_temp, bias, ih, th, p, own, sums):
    parts, losses = band(log_temp, bias, ih, th, p, True)
    for place in range(3):
        own[place] = parts[place]
        sums[place] = losses[place]


def sibling_pairs_kernel(log_temp, bias, ih, th, after, p, send):
    del after
    parts, losses = band(log_temp, bias, ih, th, p, False)
    r, width = parts[0].shape
    for place in range(3):
        send[place, pl.ds(0, r), :] = parts[place].astype(BF16)
        send[place, pl.ds(r, TAIL), :] = jnp.zeros((TAIL, width), BF16)
        send[place, pl.ds(r, TAIL), pl.ds(0, 2 * r)] = tail_of(losses[place][:1])


def spread_kernel(p_own, p_sib, t_own, t_sib, image_own, image_1, image_2, image_3):
    r = image_own.shape[0]
    n = 2 * r
    for half, (first, second) in ((1, (image_2, image_3)), (0, (image_own, image_1))):
        total = 0.0
        for p, t in ((p_own, t_own), (p_sib, t_sib)):
            total = total + lax.dot_general(
                p[pl.ds(half * n, n), :], t[pl.ds(half * r, n), :], NN, preferred_element_type=F32
            )
        first[...] = total[:r].astype(first.dtype)
        second[...] = total[r:].astype(second.dtype)


def join_kernel(own, got, sums, after, b_back, c_back):
    del after
    r = own.shape[1]
    n = sums.shape[2]
    for place, out in ((1, b_back), (2, c_back)):
        out[pl.ds(0, r), :] = (own[place] + got[place, pl.ds(0, r), :].astype(F32)).astype(BF16)
        loss = sums[place][:1] + tail_sum(got[place, pl.ds(r, TAIL), :], n)
        out[pl.ds(r, TAIL), :] = jnp.zeros((TAIL, out.shape[1]), BF16)
        out[pl.ds(r, TAIL), pl.ds(0, n)] = tail_of(loss)


def tangent(total, ref, log_temp):
    unit, scale = unit_of(ref)
    total = temper_of(log_temp, ref.shape[1]) * total
    return (total - unit * jnp.sum(unit * total, axis=-1, keepdims=True)) * scale


def image_end_kernel(log_temp, images, own, a, b, c, grad):
    total = own[...] + a[...].astype(F32) + b[...].astype(F32) + c[...].astype(F32)
    grad[...] = tangent(total, images, log_temp)


def text_end_kernel(log_temp, spot, texts, own, got, sums, b_got, c_got, grad, loss):
    r = texts.shape[0]
    n = sums.shape[2]

    def here(place):
        rows = own[place] + got[place, pl.ds(0, r), :].astype(F32)
        return rows, sums[place][:1] + tail_sum(got[place, pl.ds(r, TAIL), :], n)

    total, losses = here(0)
    more, more_losses = here(2)
    even = spot[0] < 2
    total = total + jnp.where(even, more, 0.0)
    losses = losses + jnp.where(even, more_losses, 0.0)
    for ref in (b_got, c_got):
        total = total + ref[pl.ds(0, r), :].astype(F32)
        losses = losses + tail_sum(ref[pl.ds(r, TAIL), :], n)
    grad[...] = tangent(total, texts, log_temp)
    loss[...] = losses[:, :r] / (VISITS * 4 * r)


def call(kernel, outs, name, smem, vmem, hbm=(), scratch=()):
    return pl.pallas_call(
        kernel,
        out_shape=outs,
        in_specs=[SMEM] * len(smem) + [VMEM] * len(vmem) + [HBM] * len(hbm),
        out_specs=tuple(VMEM for _ in outs),
        scratch_shapes=scratch,
        compiler_params=PARAMS,
        name=name,
    )(*smem, *vmem, *(pltpu.with_memory_space_constraint(value, pltpu.HBM) for value in hbm))


def on_device(lines, images, texts, log_temp, bias):
    r, width = images.shape
    n = 2 * r
    shape = jax.ShapeDtypeStruct
    half, long = shape((r, width), BF16), shape((r, width), F32)

    def send(value, name, **way):
        with jax.named_scope(name):
            return moved(value, lines, **way)

    log_temp, bias = jnp.reshape(log_temp, (1,)), jnp.reshape(bias, (1,))
    spot = lax.axis_index("img") % 2 * 2 + lax.axis_index("txt") // 2
    spot = jnp.reshape(spot, (1,)).astype(jnp.int32)
    c_own = send(texts, "texts_two_up", up=2, odd_only=True)
    b_own = send(texts, "texts_one_up", up=1)
    image_2 = send(images, "images_across", flip=2)
    image_3 = send(images, "images_beside_far", flip=3)
    image_1 = send(images, "images_beside", flip=1)
    ih, t_own = call(
        halves_kernel,
        (shape((4 * r, width), BF16), shape((3 * r, width), BF16)),
        "halves",
        [spot],
        [],
        [c_own, image_2, image_1, image_3, b_own, texts, images],
        scratch=(pltpu.VMEM((7, r, width), BF16), pltpu.SemaphoreType.DMA((7,))),
    )
    t_sib = send(t_own, "texts_sibling", other=1)
    slopes = shape((4 * r, n), BF16)
    p_own, own, sums = call(
        own_pairs_kernel,
        (slopes, shape((3, r, width), F32), shape((3, 8, n), F32)),
        "own_pairs",
        [log_temp, bias],
        [ih, t_own],
    )
    p_sib, text_send = call(
        sibling_pairs_kernel,
        (slopes, shape((3, r + TAIL, width), BF16)),
        "sibling_pairs",
        [log_temp, bias],
        [ih, t_sib, sums],
    )
    got = send(text_send, "text_parts_sibling", other=1)
    image_own, out_1, out_2, out_3 = call(
        spread_kernel, (long, half, half, half), "spread", [], [p_own, p_sib, t_own, t_sib]
    )
    back_2 = send(out_2, "image_parts_across", flip=2)
    back_3 = send(out_3, "image_parts_beside_far", flip=3)
    back_1 = send(out_1, "image_parts_beside", flip=1)
    back = shape((r + TAIL, width), BF16)
    b_back, c_back = call(join_kernel, (back, back), "join", [], [own, got, sums, out_2])
    c_got = send(c_back, "text_parts_two_down", up=-2, odd_only=True)
    b_got = send(b_back, "text_parts_one_down", up=-1)
    (image_grad,) = call(
        image_end_kernel, (long,), "image_end", [log_temp], [images, image_own, back_1, back_2, back_3]
    )
    text_grad, loss = call(
        text_end_kernel,
        (long, shape((1, r), F32)),
        "text_end",
        [log_temp, spot],
        [texts, own, got, sums, b_got, c_got],
    )
    return jnp.reshape(loss, (r,)), image_grad, text_grad


def solution(mesh):
    from jax.sharding import PartitionSpec as P

    lines = mesh.shape["img"] // 2
    rows = P(AXES, None)
    return jax.shard_map(
        functools.partial(on_device, lines),
        mesh=mesh,
        in_specs=(rows, rows, P(), P()),
        out_specs=(P(AXES), rows, rows),
        check_vma=False,
    )
```
